1024 devices in a mesh: pp: 16 (over y, x_lo, core), ep: 64 (over x_hi, z).
Axes of the slice: x: 4 (x_hi: 2, x_lo: 2; x = x_hi * 2 + x_lo), y: 4, z: 32, core: 2. Of those that a mesh axis runs over, the one named last changes fastest.
Arguments:
- forward_input_rows: bfloat16 [16, 2048, 7168], P('pp', 'ep'), may hold values from -6 to 6
- ids_fwd: int32 [16, 2048, 8], P('pp', 'ep'), may hold values from 0 to 255, as said below
- gate_fwd: float32 [16, 2048, 8], P('pp', 'ep'), may hold values from 0.1 to 1
- backward_input_rows: bfloat16 [16, 2048, 7168], P('pp', 'ep'), may hold values from -6 to 6
- dy_bwd: bfloat16 [16, 2048, 7168], P('pp', 'ep'), may hold values from -6 to 6
- ids_bwd: int32 [16, 2048, 8], P('pp', 'ep'), may hold values from 0 to 255, as said below
- gate_bwd: float32 [16, 2048, 8], P('pp', 'ep'), may hold values from 0.1 to 1
- saved_z: bfloat16 [16, 2, 8192, 128], P('pp', None, 'ep'), may hold values from -8 to 8
- norm_gain: float32 [16, 7168], P('pp'), may hold values from 0.25 to 1.75
- w_gate: bfloat16 [7168, 8192], P(None, 'ep'), may hold values from -0.0625 to 0.0625
- w_up: bfloat16 [7168, 8192], P(None, 'ep'), may hold values from -0.0625 to 0.0625
- w_down: bfloat16 [8192, 7168], P('ep'), may hold values from -0.125 to 0.125
Outputs:
- y_fwd: bfloat16 [16, 2048, 7168], P('pp', 'ep')
- grad_x_bwd: bfloat16 [16, 2048, 7168], P('pp', 'ep')
- grad_gate_bwd: float32 [16, 2048, 8], P('pp', 'ep')
- grad_gain: float32 [16, 64, 7168], P('pp', 'ep')
The draws below stay inside these ranges and needn't reach their ends.
Inputs may be any that keep to these rules, and one draw needn't show every extreme that they name: `ids_fwd`: each token names 8 different experts; at most one of them is below 4. Among the 32 tokens of one device at most 2 name any one expert below 4, and in every draw some expert below 4 is named by exactly 2 tokens of every device. `ids_bwd`: as for ids_fwd.
All inputs are finite; a program needn't handle non-finite values.
Results may differ from the reference program's by a relative error of at most 0.0085.
Values may be sent and summed in bfloat16 or wider, within the bound.
A program may use at most 64 MiB of HBM per device.

```python
import jax
import jax.numpy as jnp
from jax import lax

D = 7168
EXPERTS_ALL = 256
TOP = 8
HID_DEV = 128
CAP = 2
TOK_DEV = 32
SPLIT = 16
EXP_HID = 2048
EXPERTS = 4
TOKENS = 2048
N_PP = 16
N_EP = 64


def routing_draw(seed_key):
    block_count = N_PP * N_EP
    keys_all = jax.random.split(seed_key, 6)
    hot_expert = jax.random.randint(keys_all[0], (), 0, EXPERTS)
    counts = jax.random.randint(keys_all[1], (block_count, EXPERTS), 1, CAP + 1)
    counts = jnp.where(jnp.arange(EXPERTS)[None, :] == hot_expert, CAP, counts)
    orders = jax.vmap(lambda sub_key: jax.random.permutation(sub_key, TOK_DEV))(jax.random.split(keys_all[2], block_count))
    bounds = jnp.cumsum(counts, axis=1)
    positions = jnp.arange(TOK_DEV)
    expert_at = jnp.sum((positions[None, :, None] >= bounds[:, None, :]).astype(jnp.int32), axis=2)
    block_index = jnp.arange(block_count)[:, None]
    chosen = jnp.zeros((block_count, TOK_DEV), jnp.int32).at[block_index, orders].set(expert_at.astype(jnp.int32))
    others_count = EXPERTS_ALL - EXPERTS
    base_ids = jax.random.randint(keys_all[3], (block_count, TOK_DEV), 0, others_count)
    stride = jax.random.randint(keys_all[4], (block_count, TOK_DEV), 1, others_count // TOP + 1)
    spread_ids = EXPERTS + (base_ids[..., None] + jnp.arange(TOP)[None, None, :] * stride[..., None]) % others_count
    column = jax.random.randint(keys_all[5], (block_count, TOK_DEV), 0, TOP)
    use_window = (jnp.arange(TOP)[None, None, :] == column[..., None]) & (chosen[..., None] < EXPERTS)
    picks = jnp.where(use_window, chosen[..., None], spread_ids)
    return picks.reshape(N_PP, N_EP * TOK_DEV, TOP).astype(jnp.int32)


def draw_ids_fwd(key, part):
    key = jax.random.fold_in(key, 5)
    return routing_draw(key)


def draw_ids_bwd(key, part):
    key = jax.random.fold_in(key, 9)
    return routing_draw(key)


def steps_of(key, dims, shards, least, largest):
    gain = 1.0
    for dim, blocks in shards:
        draws = jax.random.uniform(jax.random.fold_in(jax.random.fold_in(key, 6), dim), (blocks,), jnp.float32, least / len(shards), largest / len(shards))
        gain = gain * jnp.repeat(jnp.exp(draws), dims[dim] // blocks).reshape((-1,) + (1,) * (len(dims) - 1 - dim))
    return gain


def centred(own_key, shape, deviation, bound, pieces=(), kind=jnp.bfloat16):
    array = deviation * jax.random.normal(own_key, shape, jnp.float32)
    if pieces:
        array = array * steps_of(own_key, shape, pieces, -0.22, 0.18)
    return jnp.clip(array, -bound, bound).astype(kind)


def setup_inputs(seed: int = 0) -> dict:
    keys = jax.random.split(jax.random.key(seed), 13)
    return {
        "forward_input_rows": centred(keys[0], (N_PP, TOKENS, D), 1.0, 6.0, ((0, 16), (1, 64))),
        "ids_fwd": draw_ids_fwd(jax.random.fold_in(keys[12], 71), 0),
        "gate_fwd": jnp.clip(0.1 + 0.9 * jax.random.uniform(keys[2], (N_PP, TOKENS, TOP), jnp.float32) ** steps_of(keys[2], (N_PP, TOKENS, TOP), ((0, 16), (1, 64)), -0.2, 0.2), 0.1, 1.0),
        "backward_input_rows": centred(keys[3], (N_PP, TOKENS, D), 1.0, 6.0, ((0, 16), (1, 64))),
        "dy_bwd": centred(keys[4], (N_PP, TOKENS, D), 1.0, 6.0, ((0, 16), (1, 64))),
        "ids_bwd": draw_ids_bwd(jax.random.fold_in(keys[12], 71), 0),
        "gate_bwd": jnp.clip(0.1 + 0.9 * jax.random.uniform(keys[6], (N_PP, TOKENS, TOP), jnp.float32) ** steps_of(keys[6], (N_PP, TOKENS, TOP), ((0, 16), (1, 64)), -0.2, 0.2), 0.1, 1.0),
        "saved_z": centred(keys[7], (N_PP, 2, N_EP * N_EP * CAP, HID_DEV), 1.5, 8.0, ((0, 16), (2, 64))),
        "norm_gain": jnp.clip(1.0 + 0.15 * jax.random.normal(keys[8], (N_PP, D), jnp.float32), 0.25, 1.75),
        "w_gate": centred(keys[9], (D, N_EP * HID_DEV), D ** -0.5, 0.0625, ((1, 64),)),
        "w_up": centred(keys[10], (D, N_EP * HID_DEV), D ** -0.5, 0.0625, ((1, 64),)),
        "w_down": centred(keys[11], (N_EP * HID_DEV, D), EXP_HID ** -0.5, 0.125, ((0, 64),)),
    }


EPSILON = 1e-06

def rebound(values):
    return lax.optimization_barrier(values.astype(jnp.bfloat16)).astype(jnp.float32)

def tables(id_rank, gate_rank):
    id_blocks = id_rank.reshape(N_EP, TOK_DEV, TOP)
    gate_blocks = gate_rank.reshape(N_EP, TOK_DEV, TOP)
    window = id_blocks < EXPERTS
    labels = jnp.arange(EXPERTS, dtype=jnp.int32)
    hit_table = jnp.any(id_blocks[..., None] == labels, axis=2).astype(jnp.int32)
    slot_rank = jnp.cumsum(hit_table, axis=1) - hit_table
    slot_ids = jnp.arange(CAP, dtype=jnp.int32)
    select = (hit_table[..., None] * (slot_rank[..., None] == slot_ids).astype(jnp.int32)).astype(jnp.float32)
    pick_gate = lax.optimization_barrier(jnp.sum(jnp.where(window, gate_blocks, jnp.zeros_like(gate_blocks)), axis=2))
    return (select, pick_gate, window)

def to_slots(select, values):
    slot_rows = jnp.einsum('ctej,ctd->ecjd', select, values.astype(jnp.float32), precision=lax.Precision.HIGHEST)
    return slot_rows.astype(jnp.bfloat16).reshape(EXPERTS, N_EP * CAP, D)

def row_norm_values(input_rows_local):
    x_float = input_rows_local.astype(jnp.float32).reshape(N_EP, TOK_DEV, D)
    inverse_root_scale = lax.rsqrt(lax.optimization_barrier(jnp.mean(x_float * x_float, axis=-1, keepdims=True)) + EPSILON)
    return (x_float * inverse_root_scale, inverse_root_scale)

def expert_columns(weights, expert_id, axis_index):
    return lax.dynamic_slice_in_dim(weights, (expert_id * EXP_HID).astype(jnp.int32), EXP_HID, axis_index)

def forward_rank(input_rows_local, id_rank, gate_rank, gain_vector_row, w_gate, w_up, w_down):
    select, pick_gate, window = tables(id_rank, gate_rank)
    centered_input_estimate, inverse_root_scale = row_norm_values(input_rows_local)
    normalized_output = (centered_input_estimate * gain_vector_row).astype(jnp.bfloat16)
    slot_rows = to_slots(select, normalized_output)
    count_rows = N_EP * CAP

    def expert(expert_id):
        rows_here = lax.dynamic_index_in_dim(slot_rows, expert_id, 0, keepdims=False)
        z_gate = jnp.dot(rows_here, expert_columns(w_gate, expert_id, 1), preferred_element_type=jnp.float32)
        z_up = jnp.dot(rows_here, expert_columns(w_up, expert_id, 1), preferred_element_type=jnp.float32)
        activation = (jax.nn.silu(z_gate) * z_up).astype(jnp.bfloat16)
        down_rows = expert_columns(w_down, expert_id, 0).reshape(SPLIT, HID_DEV, D)
        partial_value = jnp.einsum('msh,shd->msd', activation.reshape(count_rows, SPLIT, HID_DEV).astype(jnp.float32), down_rows.astype(jnp.float32))
        return lax.optimization_barrier(jnp.sum(rebound(partial_value), axis=1))
    per_slot = lax.map(expert, jnp.arange(EXPERTS, dtype=jnp.int32)).reshape(EXPERTS, N_EP, CAP, D)
    mixed_rows = pick_gate[..., None] * jnp.einsum('ctej,ecjd->ctd', select, per_slot, precision=lax.Precision.HIGHEST)
    return mixed_rows.reshape(TOKENS, D).astype(jnp.bfloat16)

def backward_rank(input_rows_local, dy_rank, id_rank, gate_rank, saved_rank, gain_vector_row, w_gate, w_up, w_down):
    select, pick_gate, window = tables(id_rank, gate_rank)
    slot_rows = to_slots(select, dy_rank.reshape(N_EP, TOK_DEV, D))
    count_rows = N_EP * CAP
    saved_split = saved_rank.reshape(2, EXPERTS, SPLIT, count_rows, HID_DEV)

    def expert(expert_id):
        rows_here = lax.dynamic_index_in_dim(slot_rows, expert_id, 0, keepdims=False)
        down_rows = expert_columns(w_down, expert_id, 0)
        grad_act = jnp.dot(rows_here, down_rows.T, preferred_element_type=jnp.float32)
        saved_here = lax.dynamic_index_in_dim(saved_split, expert_id, 1, keepdims=False)
        saved_here = jnp.transpose(saved_here, (0, 2, 1, 3)).reshape(2, count_rows, EXP_HID).astype(jnp.float32)
        pre_gate = saved_here[0]
        pre_up = saved_here[1]
        sigmoid_gate = jax.nn.sigmoid(pre_gate)
        silu_gate = pre_gate * sigmoid_gate
        activation = rebound(silu_gate * pre_up)
        grad_gate = (grad_act * pre_up * sigmoid_gate * (1.0 + pre_gate * (1.0 - sigmoid_gate))).astype(jnp.bfloat16)
        grad_up = (grad_act * silu_gate).astype(jnp.bfloat16)
        gate_cols = expert_columns(w_gate, expert_id, 1).reshape(D, SPLIT, HID_DEV).astype(jnp.float32)
        up_cols = expert_columns(w_up, expert_id, 1).reshape(D, SPLIT, HID_DEV).astype(jnp.float32)
        partial_value = jnp.einsum('msh,dsh->msd', grad_gate.reshape(count_rows, SPLIT, HID_DEV).astype(jnp.float32), gate_cols)
        partial_value = partial_value + jnp.einsum('msh,dsh->msd', grad_up.reshape(count_rows, SPLIT, HID_DEV).astype(jnp.float32), up_cols)
        part_sum = lax.optimization_barrier(jnp.sum(rebound(partial_value), axis=1))
        slot_score = lax.optimization_barrier(jnp.sum((grad_act * activation).reshape(count_rows, SPLIT, HID_DEV), axis=-1))
        return (part_sum, lax.optimization_barrier(jnp.sum(rebound(slot_score), axis=-1)))
    part_slot, score_slot = lax.map(expert, jnp.arange(EXPERTS, dtype=jnp.int32))
    part_slot = part_slot.reshape(EXPERTS, N_EP, CAP, D)
    score_slot = score_slot.reshape(EXPERTS, N_EP, CAP)
    gradient_normalized_rows = pick_gate[..., None] * jnp.einsum('ctej,ecjd->ctd', select, part_slot, precision=lax.Precision.HIGHEST)
    token_score = jnp.einsum('ctej,ecj->ct', select, score_slot, precision=lax.Precision.HIGHEST)
    grad_gate_out = jnp.where(window, token_score[..., None], jnp.zeros_like(token_score)[..., None])
    centered_input_estimate, inverse_root_scale = row_norm_values(input_rows_local)
    gain_product_term = lax.optimization_barrier(jnp.sum(gradient_normalized_rows * centered_input_estimate, axis=1))
    scaled_rows = gradient_normalized_rows * gain_vector_row
    input_gradient = inverse_root_scale * (scaled_rows - centered_input_estimate * lax.optimization_barrier(jnp.mean(scaled_rows * centered_input_estimate, axis=-1, keepdims=True)))
    return (input_gradient.reshape(TOKENS, D).astype(jnp.bfloat16), grad_gate_out.reshape(TOKENS, TOP), gain_product_term)

def reference(forward_input_rows, ids_fwd, gate_fwd, backward_input_rows, dy_bwd, ids_bwd, gate_bwd, saved_z, norm_gain, w_gate, w_up, w_down):
    y_fwd = lax.map(lambda packed: forward_rank(packed[0], packed[1], packed[2], packed[3], w_gate, w_up, w_down), (forward_input_rows, ids_fwd, gate_fwd, norm_gain))
    grad_x_bwd, grad_gate_bwd, gain_product_term = lax.map(lambda packed: backward_rank(packed[0], packed[1], packed[2], packed[3], packed[4], packed[5], w_gate, w_up, w_down), (backward_input_rows, dy_bwd, ids_bwd, gate_bwd, saved_z, norm_gain))
    grad_gain = gain_product_term + gain_product_term[::-1]
    return (y_fwd, grad_x_bwd, grad_gate_bwd, grad_gain)
```

```python
import functools

import jax
import jax.numpy as jnp
from jax import lax
from jax.experimental import pallas as pl
from jax.experimental.pallas import tpu as pltpu
from jax.sharding import PartitionSpec as P

CAP = 2
EPSILON = 1e-06
QUARTERS = 4
EXTRA = 128
MESH = pl.DeviceIdType.MESH
F32 = jnp.float32
BF16 = jnp.bfloat16


def route_tables(id_rows, gate_rows, experts):
    tokens = id_rows.shape[0]
    window = id_rows < experts
    labels = jnp.arange(experts, dtype=jnp.int32)
    hit_table = jnp.any(id_rows[:, :, None] == labels[None, None, :], axis=1).astype(F32)
    earlier = (jnp.arange(tokens)[:, None] > jnp.arange(tokens)[None, :]).astype(F32)
    slot_rank = jnp.dot(earlier, hit_table, precision=lax.Precision.HIGHEST)
    slot_ids = jnp.arange(CAP, dtype=F32)
    select = hit_table.T[:, None, :] * (slot_rank.T[:, None, :] == slot_ids[None, :, None]).astype(F32)
    pick_gate = jnp.sum(jnp.where(window, gate_rows, 0.0), axis=1)
    return (select, pick_gate, window)


def row_norm_values(x_rows):
    x_float = x_rows.astype(F32)
    inverse_root_scale = lax.rsqrt(jnp.mean(x_float * x_float, axis=-1, keepdims=True) + EPSILON)
    return (x_float * inverse_root_scale, inverse_root_scale)


def pack_rows(select, values):
    packed = jnp.einsum("ejt,td->ejd", select.astype(BF16), values, preferred_element_type=F32).astype(BF16)
    experts, slots, width = packed.shape
    folded = packed.reshape(2, 2, slots, QUARTERS, width // QUARTERS)
    return folded.transpose(0, 1, 3, 2, 4).reshape(2, 2 * QUARTERS * slots, width // QUARTERS)


def unpack_rows(folded, width):
    parts = folded.reshape(2, 2, QUARTERS, CAP, width // QUARTERS)
    return parts.transpose(0, 1, 3, 2, 4).reshape(4, CAP, width)


def to_tokens(select, per_slot):
    return jnp.einsum("ejt,ejd->td", select, per_slot.astype(F32), precision=lax.Precision.HIGHEST)


def exact_pick(chooser, rows):
    return jnp.dot(chooser, rows, preferred_element_type=F32).astype(BF16)


def ring_kernel(
    ring,
    packed_bwd,
    packed_fwd,
    saved,
    w_gate,
    w_up,
    w_down,
    out_bwd,
    out_fwd,
    gathered,
    came_x,
    acc,
    lhs,
    part_bwd,
    part_fwd,
    sums_bwd,
    sums_fwd,
    back_bwd,
    back_fwd,
    fin_bwd,
    fin_fwd,
    x_send,
    x_recv,
    g_send,
    g_recv,
    r_send,
    r_recv,
):
    half = ring // 2
    reach = half // 2
    span = half - 1 + reach
    pp = lax.axis_index("pp")
    ep = lax.axis_index("ep")
    a = ep // ring
    z = lax.rem(ep, ring)
    h = z // half
    i = lax.rem(z, half)
    quarter = packed_fwd.shape[2]
    hid = w_gate.shape[1]
    packed = (packed_bwd, packed_fwd)
    sums = (sums_bwd, sums_fwd)
    parts = (part_bwd, part_fwd)
    own_left, out_left = ring + half, ring + half + 1

    def at(position, pair=a):
        return (pp, pair * ring + lax.rem(position + 2 * ring, ring))

    partner = at(z, 1 - a)
    ways = ((1, i), (-1, half - 1 - i))

    barrier = pltpu.get_barrier_semaphore()
    for device in (at(z + 1), at(z - 1), partner):
        pl.semaphore_signal(barrier, inc=1, device_id=device, device_id_type=MESH)
    pl.semaphore_wait(barrier, 3)

    def x_copy(b):
        return pltpu.make_async_remote_copy(
            src_ref=packed[b].at[1 - a],
            dst_ref=came_x.at[b],
            send_sem=x_send.at[b],
            recv_sem=x_recv.at[b],
            device_id=partner,
            device_id_type=MESH,
        )

    for b in range(2):
        x_copy(b).start()

    def g_copy(b, source, target, sem, way):
        return pltpu.make_async_remote_copy(
            src_ref=gathered.at[b, source],
            dst_ref=gathered.at[b, target],
            send_sem=g_send.at[b, sem],
            recv_sem=g_recv.at[b, target],
            device_id=at(z + way),
            device_id_type=MESH,
        )

    def g_arrived(b, slot):
        g_copy(b, slot, slot, slot, 1).wait_recv()

    row = lax.broadcasted_iota(jnp.int32, (16, 32), 0)
    col = lax.broadcasted_iota(jnp.int32, (16, 32), 1)

    def merge(portion):
        pair = (row >> 1) & 1
        place = portion * 8 + (row >> 2) * 2 + (row & 1)
        return (col == jnp.where(pair == a, place, place + 16)).astype(BF16)

    def own_sends(b, act):
        for way, depth in ways:
            sem_in = z if way == 1 else own_left
            sem_out = ring + i if way == 1 else out_left

            @pl.when(depth < half - 1)
            def _():
                act(g_copy(b, z, z, sem_in, way))

            @pl.when(depth >= reach)
            def _():
                act(g_copy(b, ring + i, jnp.where(depth < half - 1, ring + i, z), sem_out, way))

    def begin(b):
        x_copy(b).wait_recv()
        rows = jnp.concatenate([packed[b][a], came_x[b]], axis=0)
        gathered[b, z] = exact_pick(merge(h), rows)
        gathered[b, ring + i] = exact_pick(merge(1 - h), rows)
        own_sends(b, lambda c: c.start())

    def gather_step(b, t, arrived, act):
        for way, depth in ways:
            source = lax.rem(z - way * t + ring, ring)

            @pl.when(t <= depth + reach)
            def _():
                if arrived:
                    g_arrived(b, source)

                @pl.when(depth < half - 1)
                def _():
                    act(g_copy(b, source, source, source, way))

            @pl.when(t <= depth - reach)
            def _():
                slot = ring + i - way * t
                if arrived:
                    g_arrived(b, slot)
                act(g_copy(b, slot, jnp.where(depth < half - 1, slot, source), slot, way))

    def r_copy(b, source, target, way):
        return pltpu.make_async_remote_copy(
            src_ref=sums[b].at[source],
            dst_ref=sums[b].at[target],
            send_sem=r_send.at[b, source],
            recv_sem=r_recv.at[b, target],
            device_id=at(z - way),
            device_id_type=MESH,
        )

    def r_arrived(b, slot):
        r_copy(b, slot, slot, 1).wait_recv()

    def rounded(b, total):
        if b == 1:
            return total.astype(BF16)
        score = total[0:8, quarter:] + total[8:16, quarter:]
        high = score.astype(BF16).astype(F32)
        tail = jnp.concatenate([high, score - high], axis=0)
        return jnp.concatenate([total[:, :quarter], tail], axis=1).astype(BF16)

    def reduce_target(way, depth, t, dest):
        local = jnp.where(t == 1, own_left, dest) if way == -1 else dest
        return jnp.where(depth > 0, local, ring + lax.rem(dest, half))

    def reduce_step(b, t):
        for way, depth in ways:
            dest = lax.rem(z - way * t + ring, ring)

            @pl.when(t <= depth + reach)
            def _():
                @pl.when(depth < half - 1)
                def _():
                    r_arrived(b, dest)
                    sums[b][dest] = rounded(b, sums[b][dest].astype(F32) + parts[b][dest])

                @pl.when(depth == half - 1)
                def _():
                    sums[b][dest] = rounded(b, parts[b][dest])

                r_copy(b, dest, reduce_target(way, depth, t, dest), way).start()

            @pl.when(t <= depth - reach)
            def _():
                slot = ring + i - way * t
                r_arrived(b, slot)
                r_copy(b, slot, slot, way).start()

    def reduce_drain(b, t):
        for way, depth in ways:
            dest = lax.rem(z - way * t + ring, ring)

            @pl.when(t <= depth + reach)
            def _():
                r_copy(b, dest, dest, way).wait_send()

            @pl.when(t <= depth - reach)
            def _():
                slot = ring + i - way * t
                r_copy(b, slot, slot, way).wait_send()

    rows_all = ring * 16
    row_quarter = (lax.broadcasted_iota(jnp.int32, (rows_all, 1), 0) >> 2) & 3

    def folded(value):
        width = value.shape[1]
        pairs = value.reshape(ring, 2, 8, width)
        total = pairs[:, 0] + pairs[:, 1]
        total = total + pltpu.roll(total, 4, 1)
        return total.reshape(ring * 8, width)

    def spread(value):
        width = value.shape[1]
        tiles = value.reshape(ring, 1, 8, width)
        return jnp.concatenate([tiles, tiles], axis=1).reshape(rows_all, width)

    def block(q):
        return slice(q * quarter, (q + 1) * quarter)

    nt = (((1,), (1,)), ((), ()))

    def compute_bwd():
        rows = gathered[0, 0:ring].reshape(rows_all, quarter)
        for q in range(QUARTERS):
            piece = lax.dot_general(rows, w_down[:, block(q)], nt, preferred_element_type=F32)
            acc[:, :hid] = piece if q == 0 else jnp.where(row_quarter == q, piece, acc[:, :hid])
        grad_act = folded(acc[:, :hid])
        pre_gate = saved[0]
        pre_up = saved[1]
        sig = jax.nn.sigmoid(pre_gate)
        silu = pre_gate * sig
        active = (silu * pre_up).astype(BF16).astype(F32)
        grad_gate = grad_act * pre_up * sig * (1.0 + pre_gate * (1.0 - sig))
        grad_up = grad_act * silu
        score = jnp.sum(grad_act * active, axis=1, keepdims=True)
        score = jnp.broadcast_to(score, (ring * 8, EXTRA)).reshape(ring, 8, EXTRA)
        both = spread(jnp.concatenate([grad_gate, grad_up], axis=1))
        for q in range(QUARTERS):
            lhs[:, 2 * hid * q : 2 * hid * (q + 1)] = jnp.where(row_quarter == q, both, 0.0).astype(BF16)
        part_bwd[:, 0:8, quarter:] = score
        part_bwd[:, 8:16, quarter:] = jnp.zeros_like(score)
        total = None
        for q in range(QUARTERS):
            weights = jnp.concatenate([w_gate[block(q), :], w_up[block(q), :]], axis=1)
            piece = lax.dot_general(
                lhs[:, 2 * hid * q : 2 * hid * (q + 1)], weights, nt, preferred_element_type=F32
            ).reshape(ring, 16, quarter)
            if q == 0:
                part_bwd[:, :, :quarter] = piece
            else:
                part_bwd[:, :, :quarter] += piece

    def compute_fwd():
        rows = gathered[1, 0:ring].reshape(rows_all, quarter)
        for q in range(QUARTERS):
            weights = jnp.concatenate([w_gate[block(q), :], w_up[block(q), :]], axis=1)
            piece = jnp.dot(rows, weights, preferred_element_type=F32)
            acc[...] = piece if q == 0 else jnp.where(row_quarter == q, piece, acc[...])
        z_both = folded(acc[...])
        z_gate = z_both[:, :hid]
        active = spread(z_gate * jax.nn.sigmoid(z_gate) * z_both[:, hid:])
        for q in range(QUARTERS):
            lhs[:, hid * q : hid * (q + 1)] = jnp.where(row_quarter == q, active, 0.0).astype(BF16)
        weights = jnp.concatenate([w_down[:, block(q)] for q in range(QUARTERS)], axis=0)
        part_fwd[...] = jnp.dot(
            lhs[:, : hid * QUARTERS], weights, preferred_element_type=F32
        ).reshape(ring, 16, quarter)

    for b in range(2):
        begin(b)

    @pl.loop(1, span + 1)
    def _(t):
        gather_step(0, t, True, lambda c: c.start())
        gather_step(1, t, True, lambda c: c.start())

    compute_bwd()
    compute_fwd()

    @pl.loop(0, span)
    def _(k):
        reduce_step(0, span - k)
        reduce_step(1, span - k)

    backs = (back_bwd, back_fwd)
    fins = (fin_bwd, fin_fwd)
    outs = (out_bwd, out_fwd)

    def b_copy(b):
        return pltpu.make_async_remote_copy(
            src_ref=fins[b],
            dst_ref=backs[b],
            send_sem=x_send.at[2 + b],
            recv_sem=x_recv.at[2 + b],
            device_id=partner,
            device_id_type=MESH,
        )

    def compact(pair):
        place = (row & 1) + ((row >> 1) & 3) * 4 + pair * 2
        return (col == jnp.where((row >> 3) == h, place, place + 16)).astype(BF16)

    def finish(b):
        @pl.when(i < half - 1)
        def _():
            r_arrived(b, z)
            parts[b][z] += sums[b][z].astype(F32)

        @pl.when(i > 0)
        def _():
            r_arrived(b, own_left)
            parts[b][z] += sums[b][own_left].astype(F32)

        r_arrived(b, ring + i)
        rows = jnp.concatenate([rounded(b, parts[b][z]), sums[b][ring + i]], axis=0)
        fins[b][...] = exact_pick(compact(1 - a), rows)
        b_copy(b).start()
        outs[b][a] = exact_pick(compact(a), rows)

    finish(0)
    finish(1)
    for b in range(2):
        b_copy(b).wait_recv()
        outs[b][1 - a] = backs[b][...]
        b_copy(b).wait_send()
        x_copy(b).wait_send()
        own_sends(b, lambda c: c.wait_send())

    @pl.loop(1, span + 1)
    def _(t):
        for b in range(2):
            gather_step(b, t, False, lambda c: c.wait_send())
            reduce_drain(b, t)


def exchange(packed_bwd, packed_fwd, saved, w_gate, w_up, w_down, ring):
    quarter = packed_fwd.shape[2]
    hid = w_gate.shape[1]
    wide = quarter + EXTRA
    half = ring // 2
    slots = ring + half + 2
    rows_all = ring * 16
    vmem = pl.BlockSpec(memory_space=pltpu.VMEM)
    return pl.pallas_call(
        functools.partial(ring_kernel, ring),
        out_shape=(
            jax.ShapeDtypeStruct((2, 16, wide), BF16),
            jax.ShapeDtypeStruct((2, 16, quarter), BF16),
        ),
        in_specs=[vmem] * 6,
        out_specs=(vmem, vmem),
        scratch_shapes=[
            pltpu.VMEM((2, ring + half, 16, quarter), BF16),
            pltpu.VMEM((2, 16, quarter), BF16),
            pltpu.VMEM((rows_all, 2 * hid), F32),
            pltpu.VMEM((rows_all, 2 * hid * QUARTERS), BF16),
            pltpu.VMEM((ring, 16, wide), F32),
            pltpu.VMEM((ring, 16, quarter), F32),
            pltpu.VMEM((slots, 16, wide), BF16),
            pltpu.VMEM((slots, 16, quarter), BF16),
            pltpu.VMEM((16, wide), BF16),
            pltpu.VMEM((16, quarter), BF16),
            pltpu.VMEM((16, wide), BF16),
            pltpu.VMEM((16, quarter), BF16),
            pltpu.SemaphoreType.DMA((4,)),
            pltpu.SemaphoreType.DMA((4,)),
            pltpu.SemaphoreType.DMA((2, slots)),
            pltpu.SemaphoreType.DMA((2, slots)),
            pltpu.SemaphoreType.DMA((2, slots)),
            pltpu.SemaphoreType.DMA((2, slots)),
        ],
        compiler_params=pltpu.CompilerParams(
            collective_id=0, has_side_effects=True, vmem_limit_bytes=52 * 1024 * 1024
        ),
        cost_estimate=pl.CostEstimate(
            flops=24 * ring * 4 * quarter * 4 * hid, bytes_accessed=24 * quarter * hid, transcendentals=0
        ),
    )(packed_bwd, packed_fwd, saved, w_gate, w_up, w_down)


def per_device(
    forward_input_rows,
    ids_fwd,
    gate_fwd,
    backward_input_rows,
    dy_bwd,
    ids_bwd,
    gate_bwd,
    saved_z,
    norm_gain,
    w_gate,
    w_up,
    w_down,
):
    experts = 4
    ring = lax.axis_size("ep") // 2
    gain_vector_row = norm_gain[0]
    width = forward_input_rows.shape[2]
    hid = w_gate.shape[1]
    select_b, pick_gate_b, window = route_tables(ids_bwd[0], gate_bwd[0], experts)
    packed_bwd = pack_rows(select_b, dy_bwd[0])
    select_f, pick_gate_f, _ = route_tables(ids_fwd[0], gate_fwd[0], experts)
    xhat, _ = row_norm_values(forward_input_rows[0])
    packed_fwd = pack_rows(select_f, (xhat * gain_vector_row).astype(BF16))
    saved = saved_z[0].reshape(2, 2, ring, CAP, hid).transpose(0, 2, 1, 3, 4)
    saved = jnp.broadcast_to(saved.reshape(2, ring, 1, 2 * CAP, hid), (2, ring, 2, 2 * CAP, hid))
    saved = saved.reshape(2, ring * 8, hid).astype(F32)
    back, forward = exchange(packed_bwd, packed_fwd, saved, w_gate, w_up, w_down, ring)
    quarter = width // QUARTERS
    per_slot = unpack_rows(forward, width)
    y_rows = (pick_gate_f[:, None] * to_tokens(select_f, per_slot)).astype(BF16)[None]
    score = back[:, :, quarter].reshape(2, 2, QUARTERS, CAP).astype(F32)
    score = (score[:, :, 0] + score[:, :, 2]).reshape(experts, CAP)
    token_score = jnp.einsum("ejt,ej->t", select_b, score, precision=lax.Precision.HIGHEST)
    grad_picks = jnp.where(window, token_score[:, None], 0.0)[None]
    per_slot = unpack_rows(back[:, :, :quarter], width)
    grad_normed = pick_gate_b[:, None] * to_tokens(select_b, per_slot)
    xhat, inverse = row_norm_values(backward_input_rows[0])
    gain_term = jnp.sum(grad_normed * xhat, axis=0)
    count = lax.axis_size("pp")
    mirrored = lax.ppermute(gain_term, "pp", [(p, count - 1 - p) for p in range(count)])
    scaled = grad_normed * gain_vector_row
    grad_rows = inverse * (scaled - xhat * jnp.mean(scaled * xhat, axis=-1, keepdims=True))
    return (y_rows, grad_rows.astype(BF16)[None], grad_picks, (gain_term + mirrored)[None, None])


def solution(mesh):
    rows = P("pp", "ep", None)
    return jax.shard_map(
        per_device,
        mesh=mesh,
        in_specs=(
            rows,
            rows,
            rows,
            rows,
            rows,
            rows,
            rows,
            P("pp", None, "ep", None),
            P("pp", None),
            P(None, "ep"),
            P(None, "ep"),
            P("ep", None),
        ),
        out_specs=(rows, rows, rows, rows),
        check_vma=False,
    )
```

```python
import functools

import jax
import jax.numpy as jnp
from jax import lax
from jax.experimental import pallas as pl
from jax.experimental.pallas import tpu as pltpu
from jax.sharding import PartitionSpec as P

CAP = 2
EPSILON = 1e-06
QUARTERS = 4
EXTRA = 128
MESH = pl.DeviceIdType.MESH
F32 = jnp.float32
BF16 = jnp.bfloat16


def route_tables(id_rows, gate_rows, experts):
    tokens = id_rows.shape[0]
    window = id_rows < experts
    labels = jnp.arange(experts, dtype=jnp.int32)
    hit_table = jnp.any(id_rows[:, :, None] == labels[None, None, :], axis=1).astype(F32)
    earlier = (jnp.arange(tokens)[:, None] > jnp.arange(tokens)[None, :]).astype(F32)
    slot_rank = jnp.dot(earlier, hit_table, precision=lax.Precision.HIGHEST)
    slot_ids = jnp.arange(CAP, dtype=F32)
    select = hit_table.T[:, None, :] * (slot_rank.T[:, None, :] == slot_ids[None, :, None]).astype(F32)
    pick_gate = jnp.sum(jnp.where(window, gate_rows, 0.0), axis=1)
    return (select, pick_gate, window)


def row_norm_values(x_rows):
    x_float = x_rows.astype(F32)
    inverse_root_scale = lax.rsqrt(jnp.mean(x_float * x_float, axis=-1, keepdims=True) + EPSILON)
    return (x_float * inverse_root_scale, inverse_root_scale)


def pack_rows(select, values):
    packed = jnp.einsum("ejt,td->ejd", select.astype(BF16), values, preferred_element_type=F32).astype(BF16)
    experts, slots, width = packed.shape
    folded = packed.reshape(2, 2, slots, QUARTERS, width // QUARTERS)
    return folded.transpose(0, 1, 3, 2, 4).reshape(2, 2 * QUARTERS * slots, width // QUARTERS)


def unpack_rows(folded, width):
    parts = folded.reshape(2, 2, QUARTERS, CAP, width // QUARTERS)
    return parts.transpose(0, 1, 3, 2, 4).reshape(4, CAP, width)


def to_tokens(select, per_slot):
    return jnp.einsum("ejt,ejd->td", select, per_slot.astype(F32), precision=lax.Precision.HIGHEST)


def exact_pick(chooser, rows):
    return jnp.dot(chooser, rows, preferred_element_type=F32).astype(BF16)


def ring_kernel(
    ring,
    packed_bwd,
    packed_fwd,
    saved,
    w_gate,
    w_up,
    w_down,
    out_bwd,
    out_fwd,
    gathered,
    came_x,
    acc,
    lhs,
    part_bwd,
    part_fwd,
    sums_bwd,
    sums_fwd,
    back_bwd,
    back_fwd,
    fin_bwd,
    fin_fwd,
    x_send,
    x_recv,
    g_send,
    g_recv,
    r_send,
    r_recv,
):
    half = ring // 2
    pp = lax.axis_index("pp")
    ep = lax.axis_index("ep")
    a = ep // ring
    z = lax.rem(ep, ring)
    h = z // half
    i = lax.rem(z, half)
    quarter = packed_fwd.shape[2]
    hid = w_gate.shape[1]
    packed = (packed_bwd, packed_fwd)
    sums = (sums_bwd, sums_fwd)
    parts = (part_bwd, part_fwd)
    own_left, out_left = ring + half, ring + half + 1

    def at(position, pair=a):
        return (pp, pair * ring + lax.rem(position + 2 * ring, ring))

    partner = at(z, 1 - a)
    ways = ((1, i, half), (-1, half - 1 - i, half - 1))

    barrier = pltpu.get_barrier_semaphore()
    for device in (at(z + 1), at(z - 1), partner):
        pl.semaphore_signal(barrier, inc=1, device_id=device, device_id_type=MESH)
    pl.semaphore_wait(barrier, 3)

    def x_copy(b):
        return pltpu.make_async_remote_copy(
            src_ref=packed[b].at[1 - a],
            dst_ref=came_x.at[b],
            send_sem=x_send.at[b],
            recv_sem=x_recv.at[b],
            device_id=partner,
            device_id_type=MESH,
        )

    for b in range(2):
        x_copy(b).start()

    def g_copy(b, source, target, sem, way):
        return pltpu.make_async_remote_copy(
            src_ref=gathered.at[b, source],
            dst_ref=gathered.at[b, target],
            send_sem=g_send.at[b, sem],
            recv_sem=g_recv.at[b, target],
            device_id=at(z + way),
            device_id_type=MESH,
        )

    def g_arrived(b, slot):
        g_copy(b, slot, slot, slot, 1).wait_recv()

    row = lax.broadcasted_iota(jnp.int32, (16, 32), 0)
    col = lax.broadcasted_iota(jnp.int32, (16, 32), 1)

    def merge(portion):
        pair = (row >> 1) & 1
        place = portion * 8 + (row >> 2) * 2 + (row & 1)
        return (col == jnp.where(pair == a, place, place + 16)).astype(BF16)

    def own_sends(b, act):
        for way, depth, reach in ways:
            sem_in = z if way == 1 else own_left
            sem_out = ring + i if way == 1 else out_left

            @pl.when(depth < half - 1)
            def _():
                act(g_copy(b, z, z, sem_in, way))

            @pl.when(depth >= half - reach)
            def _():
                act(g_copy(b, ring + i, jnp.where(depth < half - 1, ring + i, z), sem_out, way))

    def begin(b):
        x_copy(b).wait_recv()
        rows = jnp.concatenate([packed[b][a], came_x[b]], axis=0)
        gathered[b, z] = exact_pick(merge(h), rows)
        gathered[b, ring + i] = exact_pick(merge(1 - h), rows)
        own_sends(b, lambda c: c.start())

    def gather_step(b, t, arrived, act):
        for way, depth, reach in ways:
            source = lax.rem(z - way * t + ring, ring)

            @pl.when((t < reach) & (depth < half - 1))
            def _():
                if arrived:
                    g_arrived(b, source)
                act(g_copy(b, source, source, source, way))

            @pl.when(t <= depth - half + reach)
            def _():
                slot = ring + i - way * t
                if arrived:
                    g_arrived(b, slot)
                act(g_copy(b, slot, jnp.where(depth < half - 1, slot, source), slot, way))

    def gather_rest(b):
        for way, depth, reach in ways:

            @pl.when(depth < half - 1)
            def _():
                g_arrived(b, lax.rem(z - way * reach + ring, ring))

            @pl.when(depth == half - 1)
            def _():
                @pl.loop(1, reach + 1)
                def _(t):
                    g_arrived(b, lax.rem(z - way * t + ring, ring))

    def r_copy(b, source, target, way):
        return pltpu.make_async_remote_copy(
            src_ref=sums[b].at[source],
            dst_ref=sums[b].at[target],
            send_sem=r_send.at[b, source],
            recv_sem=r_recv.at[b, target],
            device_id=at(z - way),
            device_id_type=MESH,
        )

    def r_arrived(b, slot):
        r_copy(b, slot, slot, 1).wait_recv()

    def rounded(b, total):
        if b == 1:
            return total.astype(BF16)
        score = total[0:8, quarter:] + total[8:16, quarter:]
        high = score.astype(BF16).astype(F32)
        tail = jnp.concatenate([high, score - high], axis=0)
        return jnp.concatenate([total[:, :quarter], tail], axis=1).astype(BF16)

    def reduce_step(b, t):
        for way, depth, reach in ways:
            dest = lax.rem(z - way * t + ring, ring)
            local, other = dest, ring + lax.rem(dest, half)
            if way == -1:
                local = jnp.where(t == 1, own_left, local)
                other = jnp.where(t == 1, out_left, other)

            @pl.when(t <= reach)
            def _():
                chained = (t < reach) & (depth < half - 1)

                @pl.when(chained)
                def _():
                    r_arrived(b, dest)
                    sums[b][dest] = rounded(b, sums[b][dest].astype(F32) + parts[b][dest])

                @pl.when(jnp.logical_not(chained))
                def _():
                    sums[b][dest] = rounded(b, parts[b][dest])

                r_copy(b, dest, jnp.where(depth > 0, local, other), way).start()

            @pl.when(t <= depth - half + reach)
            def _():
                slot = ring + i - way * t
                r_arrived(b, slot)
                r_copy(b, slot, other, way).start()

    def reduce_drain(b, t):
        for way, depth, reach in ways:
            dest = lax.rem(z - way * t + ring, ring)

            @pl.when(t <= reach)
            def _():
                r_copy(b, dest, dest, way).wait_send()

            @pl.when(t <= depth - half + reach)
            def _():
                slot = ring + i - way * t
                r_copy(b, slot, slot, way).wait_send()

    rows_all = ring * 16
    row_quarter = (lax.broadcasted_iota(jnp.int32, (rows_all, 1), 0) >> 2) & 3

    def folded(value):
        width = value.shape[1]
        pairs = value.reshape(ring, 2, 8, width)
        total = pairs[:, 0] + pairs[:, 1]
        total = total + pltpu.roll(total, 4, 1)
        return total.reshape(ring * 8, width)

    def spread(value):
        width = value.shape[1]
        tiles = value.reshape(ring, 1, 8, width)
        return jnp.concatenate([tiles, tiles], axis=1).reshape(rows_all, width)

    def block(q):
        return slice(q * quarter, (q + 1) * quarter)

    nt = (((1,), (1,)), ((), ()))

    def compute_bwd():
        rows = gathered[0, 0:ring].reshape(rows_all, quarter)
        for q in range(QUARTERS):
            piece = lax.dot_general(rows, w_down[:, block(q)], nt, preferred_element_type=F32)
            acc[:, :hid] = piece if q == 0 else jnp.where(row_quarter == q, piece, acc[:, :hid])
        grad_act = folded(acc[:, :hid])
        pre_gate = saved[0]
        pre_up = saved[1]
        sig = jax.nn.sigmoid(pre_gate)
        silu = pre_gate * sig
        active = (silu * pre_up).astype(BF16).astype(F32)
        grad_gate = grad_act * pre_up * sig * (1.0 + pre_gate * (1.0 - sig))
        grad_up = grad_act * silu
        score = jnp.sum(grad_act * active, axis=1, keepdims=True)
        score = jnp.broadcast_to(score, (ring * 8, EXTRA)).reshape(ring, 8, EXTRA)
        both = spread(jnp.concatenate([grad_gate, grad_up], axis=1))
        for q in range(QUARTERS):
            lhs[:, 2 * hid * q : 2 * hid * (q + 1)] = jnp.where(row_quarter == q, both, 0.0).astype(BF16)
        part_bwd[:, 0:8, quarter:] = score
        part_bwd[:, 8:16, quarter:] = jnp.zeros_like(score)
        for q in range(QUARTERS):
            weights = jnp.concatenate([w_gate[block(q), :], w_up[block(q), :]], axis=1)
            piece = lax.dot_general(
                lhs[:, 2 * hid * q : 2 * hid * (q + 1)], weights, nt, preferred_element_type=F32
            ).reshape(ring, 16, quarter)
            if q == 0:
                part_bwd[:, :, :quarter] = piece
            else:
                part_bwd[:, :, :quarter] += piece

    def compute_fwd():
        rows = gathered[1, 0:ring].reshape(rows_all, quarter)
        for q in range(QUARTERS):
            weights = jnp.concatenate([w_gate[block(q), :], w_up[block(q), :]], axis=1)
            piece = jnp.dot(rows, weights, preferred_element_type=F32)
            acc[...] = piece if q == 0 else jnp.where(row_quarter == q, piece, acc[...])
        z_both = folded(acc[...])
        z_gate = z_both[:, :hid]
        active = spread(z_gate * jax.nn.sigmoid(z_gate) * z_both[:, hid:])
        for q in range(QUARTERS):
            lhs[:, hid * q : hid * (q + 1)] = jnp.where(row_quarter == q, active, 0.0).astype(BF16)
        weights = jnp.concatenate([w_down[:, block(q)] for q in range(QUARTERS)], axis=0)
        part_fwd[...] = jnp.dot(
            lhs[:, : hid * QUARTERS], weights, preferred_element_type=F32
        ).reshape(ring, 16, quarter)

    begin(0)
    begin(1)

    def send(copy):
        copy.start()

    gather_step(0, 1, True, send)

    @pl.loop(1, half)
    def _(t):
        gather_step(1, t, True, send)
        gather_step(0, t + 1, True, send)

    gather_rest(0)
    compute_bwd()
    gather_step(1, half, True, send)
    reduce_step(0, half)
    gather_rest(1)
    compute_fwd()

    @pl.loop(0, half - 1)
    def _(k):
        reduce_step(1, half - k)
        reduce_step(0, half - 1 - k)

    reduce_step(1, 1)

    backs = (back_bwd, back_fwd)
    fins = (fin_bwd, fin_fwd)
    outs = (out_bwd, out_fwd)

    def b_copy(b):
        return pltpu.make_async_remote_copy(
            src_ref=fins[b],
            dst_ref=backs[b],
            send_sem=x_send.at[2 + b],
            recv_sem=x_recv.at[2 + b],
            device_id=partner,
            device_id_type=MESH,
        )

    def compact(pair):
        place = (row & 1) + ((row >> 1) & 3) * 4 + pair * 2
        return (col == jnp.where((row >> 3) == h, place, place + 16)).astype(BF16)

    def finish(b):
        @pl.when(i < half - 1)
        def _():
            r_arrived(b, z)
            parts[b][z] += sums[b][z].astype(F32)

        @pl.when(i > 0)
        def _():
            r_arrived(b, own_left)
            parts[b][z] += sums[b][own_left].astype(F32)

        r_arrived(b, ring + i)

        @pl.when(i < half - 1)
        def _():
            r_arrived(b, out_left)
            added = sums[b][ring + i].astype(F32) + sums[b][out_left].astype(F32)
            sums[b][ring + i] = rounded(b, added)

        rows = jnp.concatenate([rounded(b, parts[b][z]), sums[b][ring + i]], axis=0)
        fins[b][...] = exact_pick(compact(1 - a), rows)
        b_copy(b).start()
        outs[b][a] = exact_pick(compact(a), rows)

    finish(0)
    finish(1)
    for b in range(2):
        b_copy(b).wait_recv()
        outs[b][1 - a] = backs[b][...]
        b_copy(b).wait_send()
        x_copy(b).wait_send()
        own_sends(b, lambda c: c.wait_send())

    @pl.loop(1, half + 1)
    def _(t):
        for b in range(2):
            gather_step(b, t, False, lambda c: c.wait_send())
            reduce_drain(b, t)


def exchange(packed_bwd, packed_fwd, saved, w_gate, w_up, w_down, ring):
    quarter = packed_fwd.shape[2]
    hid = w_gate.shape[1]
    wide = quarter + EXTRA
    half = ring // 2
    slots = ring + half + 2
    rows_all = ring * 16
    vmem = pl.BlockSpec(memory_space=pltpu.VMEM)
    return pl.pallas_call(
        functools.partial(ring_kernel, ring),
        out_shape=(
            jax.ShapeDtypeStruct((2, 16, wide), BF16),
            jax.ShapeDtypeStruct((2, 16, quarter), BF16),
        ),
        in_specs=[vmem] * 6,
        out_specs=(vmem, vmem),
        scratch_shapes=[
            pltpu.VMEM((2, ring + half, 16, quarter), BF16),
            pltpu.VMEM((2, 16, quarter), BF16),
            pltpu.VMEM((rows_all, 2 * hid), F32),
            pltpu.VMEM((rows_all, 2 * hid * QUARTERS), BF16),
            pltpu.VMEM((ring, 16, wide), F32),
            pltpu.VMEM((ring, 16, quarter), F32),
            pltpu.VMEM((slots, 16, wide), BF16),
            pltpu.VMEM((slots, 16, quarter), BF16),
            pltpu.VMEM((16, wide), BF16),
            pltpu.VMEM((16, quarter), BF16),
            pltpu.VMEM((16, wide), BF16),
            pltpu.VMEM((16, quarter), BF16),
            pltpu.SemaphoreType.DMA((4,)),
            pltpu.SemaphoreType.DMA((4,)),
            pltpu.SemaphoreType.DMA((2, slots)),
            pltpu.SemaphoreType.DMA((2, slots)),
            pltpu.SemaphoreType.DMA((2, slots)),
            pltpu.SemaphoreType.DMA((2, slots)),
        ],
        compiler_params=pltpu.CompilerParams(
            collective_id=0, has_side_effects=True, vmem_limit_bytes=52 * 1024 * 1024
        ),
        cost_estimate=pl.CostEstimate(
            flops=24 * ring * 4 * quarter * 4 * hid, bytes_accessed=24 * quarter * hid, transcendentals=0
        ),
    )(packed_bwd, packed_fwd, saved, w_gate, w_up, w_down)


def per_device(
    forward_input_rows,
    ids_fwd,
    gate_fwd,
    backward_input_rows,
    dy_bwd,
    ids_bwd,
    gate_bwd,
    saved_z,
    norm_gain,
    w_gate,
    w_up,
    w_down,
):
    experts = 4
    ring = lax.axis_size("ep") // 2
    gain_vector_row = norm_gain[0]
    width = forward_input_rows.shape[2]
    hid = w_gate.shape[1]
    select_b, pick_gate_b, window = route_tables(ids_bwd[0], gate_bwd[0], experts)
    packed_bwd = pack_rows(select_b, dy_bwd[0])
    select_f, pick_gate_f, _ = route_tables(ids_fwd[0], gate_fwd[0], experts)
    xhat, _ = row_norm_values(forward_input_rows[0])
    packed_fwd = pack_rows(select_f, (xhat * gain_vector_row).astype(BF16))
    saved = saved_z[0].reshape(2, 2, ring, CAP, hid).transpose(0, 2, 1, 3, 4)
    saved = jnp.broadcast_to(saved.reshape(2, ring, 1, 2 * CAP, hid), (2, ring, 2, 2 * CAP, hid))
    saved = saved.reshape(2, ring * 8, hid).astype(F32)
    back, forward = exchange(packed_bwd, packed_fwd, saved, w_gate, w_up, w_down, ring)
    quarter = width // QUARTERS
    per_slot = unpack_rows(forward, width)
    y_rows = (pick_gate_f[:, None] * to_tokens(select_f, per_slot)).astype(BF16)[None]
    score = back[:, :, quarter].reshape(2, 2, QUARTERS, CAP).astype(F32)
    score = (score[:, :, 0] + score[:, :, 2]).reshape(experts, CAP)
    token_score = jnp.einsum("ejt,ej->t", select_b, score, precision=lax.Precision.HIGHEST)
    grad_picks = jnp.where(window, token_score[:, None], 0.0)[None]
    per_slot = unpack_rows(back[:, :, :quarter], width)
    grad_normed = pick_gate_b[:, None] * to_tokens(select_b, per_slot)
    xhat, inverse = row_norm_values(backward_input_rows[0])
    gain_term = jnp.sum(grad_normed * xhat, axis=0)
    count = lax.axis_size("pp")
    mirrored = lax.ppermute(gain_term, "pp", [(p, count - 1 - p) for p in range(count)])
    scaled = grad_normed * gain_vector_row
    grad_rows = inverse * (scaled - xhat * jnp.mean(scaled * xhat, axis=-1, keepdims=True))
    return (y_rows, grad_rows.astype(BF16)[None], grad_picks, (gain_term + mirrored)[None, None])


def solution(mesh):
    rows = P("pp", "ep", None)
    return jax.shard_map(
        per_device,
        mesh=mesh,
        in_specs=(
            rows,
            rows,
            rows,
            rows,
            rows,
            rows,
            rows,
            P("pp", None, "ep", None),
            P("pp", None),
            P(None, "ep"),
            P(None, "ep"),
            P("ep", None),
        ),
        out_specs=(rows, rows, rows, rows),
        check_vma=False,
    )
```

```python
import functools

import jax
import jax.numpy as jnp
from jax import lax
from jax.experimental import pallas as pl
from jax.experimental.pallas import tpu as pltpu
from jax.sharding import PartitionSpec as P

CAP = 2
EPSILON = 1e-06
QUARTERS = 4
EXTRA = 128
MESH = pl.DeviceIdType.MESH
F32 = jnp.float32
BF16 = jnp.bfloat16


def route_tables(id_rows, gate_rows, experts):
    tokens = id_rows.shape[0]
    window = id_rows < experts
    labels = jnp.arange(experts, dtype=jnp.int32)
    hit_table = jnp.any(id_rows[:, :, None] == labels[None, None, :], axis=1).astype(F32)
    earlier = (jnp.arange(tokens)[:, None] > jnp.arange(tokens)[None, :]).astype(F32)
    slot_rank = jnp.dot(earlier, hit_table, precision=lax.Precision.HIGHEST)
    slot_ids = jnp.arange(CAP, dtype=F32)
    select = hit_table.T[:, None, :] * (slot_rank.T[:, None, :] == slot_ids[None, :, None]).astype(F32)
    pick_gate = jnp.sum(jnp.where(window, gate_rows, 0.0), axis=1)
    return (select, pick_gate, window)


def row_norm_values(x_rows):
    x_float = x_rows.astype(F32)
    inverse_root_scale = lax.rsqrt(jnp.mean(x_float * x_float, axis=-1, keepdims=True) + EPSILON)
    return (x_float * inverse_root_scale, inverse_root_scale)


def pack_rows(select, values):
    packed = jnp.einsum("ejt,td->ejd", select.astype(BF16), values, preferred_element_type=F32).astype(BF16)
    experts, slots, width = packed.shape
    folded = packed.reshape(2, 2, slots, QUARTERS, width // QUARTERS)
    return folded.transpose(0, 1, 3, 2, 4).reshape(2, 2 * QUARTERS * slots, width // QUARTERS)


def slot_picks(select):
    experts, slots, tokens = select.shape
    picks = jnp.broadcast_to(select[:, None], (experts, QUARTERS, slots, tokens))
    return picks.reshape(experts * QUARTERS * slots, tokens).T


def exact_pick(chooser, rows):
    return jnp.dot(chooser, rows, preferred_element_type=F32).astype(BF16)


def ring_kernel(
    ring,
    packed_bwd,
    packed_fwd,
    saved,
    w_gate,
    w_up,
    w_down,
    x_bwd,
    gain,
    pick_bwd,
    pick_fwd,
    scale_bwd,
    scale_fwd,
    y_out,
    grad_x,
    score_out,
    gain_out,
    out_bwd,
    out_fwd,
    gain_own,
    gain_came,
    inverse,
    gathered,
    came_x,
    acc,
    lhs,
    part_bwd,
    part_fwd,
    sums_bwd,
    sums_fwd,
    back_bwd,
    back_fwd,
    fin_bwd,
    fin_fwd,
    x_send,
    x_recv,
    g_send,
    g_recv,
    r_send,
    r_recv,
):
    half = ring // 2
    pp = lax.axis_index("pp")
    ep = lax.axis_index("ep")
    a = ep // ring
    z = lax.rem(ep, ring)
    h = z // half
    i = lax.rem(z, half)
    quarter = packed_fwd.shape[2]
    hid = w_gate.shape[1]
    packed = (packed_bwd, packed_fwd)
    sums = (sums_bwd, sums_fwd)
    parts = (part_bwd, part_fwd)
    own_left, out_left = ring + half, ring + half + 1

    def at(position, pair=a):
        return (pp, pair * ring + lax.rem(position + 2 * ring, ring))

    partner = at(z, 1 - a)
    ways = (
        ((1, i, half), (-1, half - 1 - i, half - 1)),
        ((1, i, half - 1), (-1, half - 1 - i, half)),
    )

    barrier = pltpu.get_barrier_semaphore()
    pairs = lax.axis_size("pp")
    mirror = (pairs - 1 - pp, ep)
    for device in (at(z + 1), at(z - 1), partner) + ((mirror,) if pairs > 1 else ()):
        pl.semaphore_signal(barrier, inc=1, device_id=device, device_id_type=MESH)
    pl.semaphore_wait(barrier, 4 if pairs > 1 else 3)

    def x_copy(b):
        return pltpu.make_async_remote_copy(
            src_ref=packed[b].at[1 - a],
            dst_ref=came_x.at[b],
            send_sem=x_send.at[b],
            recv_sem=x_recv.at[b],
            device_id=partner,
            device_id_type=MESH,
        )

    for b in range(2):
        x_copy(b).start()

    def g_copy(b, source, target, sem, way):
        return pltpu.make_async_remote_copy(
            src_ref=gathered.at[b, source],
            dst_ref=gathered.at[b, target],
            send_sem=g_send.at[b, sem],
            recv_sem=g_recv.at[b, target],
            device_id=at(z + way),
            device_id_type=MESH,
        )

    def g_arrived(b, slot):
        g_copy(b, slot, slot, slot, 1).wait_recv()

    row = lax.broadcasted_iota(jnp.int32, (16, 32), 0)
    col = lax.broadcasted_iota(jnp.int32, (16, 32), 1)

    def merge(portion):
        pair = (row >> 1) & 1
        place = portion * 8 + (row >> 2) * 2 + (row & 1)
        return (col == jnp.where(pair == a, place, place + 16)).astype(BF16)

    def own_sends(b, act):
        for way, depth, reach in ways[b]:
            sem_in = z if way == 1 else own_left
            sem_out = ring + i if way == 1 else out_left

            @pl.when(depth < half - 1)
            def _():
                act(g_copy(b, z, z, sem_in, way))

            @pl.when(depth >= half - reach)
            def _():
                act(g_copy(b, ring + i, jnp.where(depth < half - 1, ring + i, z), sem_out, way))

    def begin(b):
        x_copy(b).wait_recv()
        rows = jnp.concatenate([packed[b][a], came_x[b]], axis=0)
        gathered[b, z] = exact_pick(merge(h), rows)
        gathered[b, ring + i] = exact_pick(merge(1 - h), rows)
        own_sends(b, lambda c: c.start())

    def gather_step(b, t, arrived, act):
        for way, depth, reach in ways[b]:
            source = lax.rem(z - way * t + ring, ring)

            @pl.when((t < reach) & (depth < half - 1))
            def _():
                if arrived:
                    g_arrived(b, source)
                act(g_copy(b, source, source, source, way))

            @pl.when(t <= depth - half + reach)
            def _():
                slot = ring + i - way * t
                if arrived:
                    g_arrived(b, slot)
                act(g_copy(b, slot, jnp.where(depth < half - 1, slot, source), slot, way))

    def gather_rest(b):
        for way, depth, reach in ways[b]:

            @pl.when(depth < half - 1)
            def _():
                g_arrived(b, lax.rem(z - way * reach + ring, ring))

            @pl.when(depth == half - 1)
            def _():
                @pl.loop(1, reach + 1)
                def _(t):
                    g_arrived(b, lax.rem(z - way * t + ring, ring))

    def r_copy(b, source, target, way):
        return pltpu.make_async_remote_copy(
            src_ref=sums[b].at[source],
            dst_ref=sums[b].at[target],
            send_sem=r_send.at[b, source],
            recv_sem=r_recv.at[b, target],
            device_id=at(z - way),
            device_id_type=MESH,
        )

    def r_arrived(b, slot):
        r_copy(b, slot, slot, 1).wait_recv()

    def rounded(b, total):
        if b == 1:
            return total.astype(BF16)
        score = total[0:8, quarter:] + total[8:16, quarter:]
        high = score.astype(BF16).astype(F32)
        tail = jnp.concatenate([high, score - high], axis=0)
        return jnp.concatenate([total[:, :quarter], tail], axis=1).astype(BF16)

    def reduce_step(b, t):
        for way, depth, reach in ways[b]:
            dest = lax.rem(z - way * t + ring, ring)
            local, other = dest, ring + lax.rem(dest, half)
            if way == -1:
                local = jnp.where(t == 1, own_left, local)
                other = jnp.where(t == 1, out_left, other)

            @pl.when(t <= reach)
            def _():
                chained = (t < reach) & (depth < half - 1)

                @pl.when(chained)
                def _():
                    r_arrived(b, dest)
                    sums[b][dest] = rounded(b, sums[b][dest].astype(F32) + parts[b][dest])

                @pl.when(jnp.logical_not(chained))
                def _():
                    sums[b][dest] = rounded(b, parts[b][dest])

                r_copy(b, dest, jnp.where(depth > 0, local, other), way).start()

            @pl.when(t <= depth - half + reach)
            def _():
                slot = ring + i - way * t
                r_arrived(b, slot)
                r_copy(b, slot, other, way).start()

    def reduce_drain(b, t):
        for way, depth, reach in ways[b]:
            dest = lax.rem(z - way * t + ring, ring)

            @pl.when(t <= reach)
            def _():
                r_copy(b, dest, dest, way).wait_send()

            @pl.when(t <= depth - half + reach)
            def _():
                slot = ring + i - way * t
                r_copy(b, slot, slot, way).wait_send()

    rows_all = ring * 16
    row_quarter = (lax.broadcasted_iota(jnp.int32, (rows_all, 1), 0) >> 2) & 3

    def folded(value):
        width = value.shape[1]
        pairs = value.reshape(ring, 2, 8, width)
        total = pairs[:, 0] + pairs[:, 1]
        total = total + pltpu.roll(total, 4, 1)
        return total.reshape(ring * 8, width)

    def spread(value):
        width = value.shape[1]
        tiles = value.reshape(ring, 1, 8, width)
        return jnp.concatenate([tiles, tiles], axis=1).reshape(rows_all, width)

    def block(q):
        return slice(q * quarter, (q + 1) * quarter)

    nt = (((1,), (1,)), ((), ()))

    def compute_bwd():
        rows = gathered[0, 0:ring].reshape(rows_all, quarter)
        for q in range(QUARTERS):
            piece = lax.dot_general(rows, w_down[:, block(q)], nt, preferred_element_type=F32)
            acc[:, :hid] = piece if q == 0 else jnp.where(row_quarter == q, piece, acc[:, :hid])
        grad_act = folded(acc[:, :hid])
        pre_gate = saved[0]
        pre_up = saved[1]
        sig = jax.nn.sigmoid(pre_gate)
        silu = pre_gate * sig
        active = (silu * pre_up).astype(BF16).astype(F32)
        grad_gate = grad_act * pre_up * sig * (1.0 + pre_gate * (1.0 - sig))
        grad_up = grad_act * silu
        score = jnp.sum(grad_act * active, axis=1, keepdims=True)
        score = jnp.broadcast_to(score, (ring * 8, EXTRA)).reshape(ring, 8, EXTRA)
        both = spread(jnp.concatenate([grad_gate, grad_up], axis=1))
        for q in range(QUARTERS):
            lhs[:, 2 * hid * q : 2 * hid * (q + 1)] = jnp.where(row_quarter == q, both, 0.0).astype(BF16)
        part_bwd[:, 0:8, quarter:] = score
        part_bwd[:, 8:16, quarter:] = jnp.zeros_like(score)
        for q in range(QUARTERS):
            weights = jnp.concatenate([w_gate[block(q), :], w_up[block(q), :]], axis=1)
            piece = lax.dot_general(
                lhs[:, 2 * hid * q : 2 * hid * (q + 1)], weights, nt, preferred_element_type=F32
            ).reshape(ring, 16, quarter)
            if q == 0:
                part_bwd[:, :, :quarter] = piece
            else:
                part_bwd[:, :, :quarter] += piece

    def compute_fwd():
        rows = gathered[1, 0:ring].reshape(rows_all, quarter)
        for q in range(QUARTERS):
            weights = jnp.concatenate([w_gate[block(q), :], w_up[block(q), :]], axis=1)
            piece = jnp.dot(rows, weights, preferred_element_type=F32)
            acc[...] = piece if q == 0 else jnp.where(row_quarter == q, piece, acc[...])
        z_both = folded(acc[...])
        z_gate = z_both[:, :hid]
        active = spread(z_gate * jax.nn.sigmoid(z_gate) * z_both[:, hid:])
        for q in range(QUARTERS):
            lhs[:, hid * q : hid * (q + 1)] = jnp.where(row_quarter == q, active, 0.0).astype(BF16)
        weights = jnp.concatenate([w_down[:, block(q)] for q in range(QUARTERS)], axis=0)
        part_fwd[...] = jnp.dot(
            lhs[:, : hid * QUARTERS], weights, preferred_element_type=F32
        ).reshape(ring, 16, quarter)

    squares = jnp.zeros((x_bwd.shape[0], 1), F32)
    for q in range(QUARTERS):
        piece = x_bwd[:, block(q)].astype(F32)
        squares += jnp.sum(piece * piece, axis=1, keepdims=True)
    inverse[...] = jnp.broadcast_to(lax.rsqrt(squares / (QUARTERS * quarter) + EPSILON), inverse.shape)
    begin(0)
    begin(1)

    def send(copy):
        copy.start()

    gather_step(0, 1, True, send)

    @pl.loop(1, half)
    def _(t):
        gather_step(1, t, True, send)
        gather_step(0, t + 1, True, send)

    gather_rest(0)
    compute_bwd()
    gather_step(1, half, True, send)
    reduce_step(0, half)
    gather_rest(1)
    compute_fwd()

    @pl.loop(0, half - 1)
    def _(k):
        reduce_step(1, half - k)
        reduce_step(0, half - 1 - k)

    reduce_step(1, 1)

    backs = (back_bwd, back_fwd)
    fins = (fin_bwd, fin_fwd)
    outs = (out_bwd, out_fwd)

    def b_copy(b):
        return pltpu.make_async_remote_copy(
            src_ref=fins[b],
            dst_ref=backs[b],
            send_sem=x_send.at[2 + b],
            recv_sem=x_recv.at[2 + b],
            device_id=partner,
            device_id_type=MESH,
        )

    def compact(pair):
        place = (row & 1) + ((row >> 1) & 3) * 4 + pair * 2
        return (col == jnp.where((row >> 3) == h, place, place + 16)).astype(BF16)

    def finish(b):
        @pl.when(i < half - 1)
        def _():
            r_arrived(b, z)
            parts[b][z] += sums[b][z].astype(F32)

        @pl.when(i > 0)
        def _():
            r_arrived(b, own_left)
            parts[b][z] += sums[b][own_left].astype(F32)

        if b == 0:
            first, second, both = ring + i, out_left, i < half - 1
        else:
            first, second, both = out_left, ring + i, i > 0
        r_arrived(b, first)

        @pl.when(both)
        def _():
            r_arrived(b, second)
            added = sums[b][first].astype(F32) + sums[b][second].astype(F32)
            sums[b][first] = rounded(b, added)

        rows = jnp.concatenate([rounded(b, parts[b][z]), sums[b][first]], axis=0)
        fins[b][...] = exact_pick(compact(1 - a), rows)
        b_copy(b).start()
        outs[b][a] = exact_pick(compact(a), rows)

    def m_copy():
        return pltpu.make_async_remote_copy(
            src_ref=gain_own,
            dst_ref=gain_came,
            send_sem=x_send.at[4],
            recv_sem=x_recv.at[4],
            device_id=mirror,
            device_id_type=MESH,
        )

    lane = lax.broadcasted_iota(jnp.int32, (1, 32), 1)

    def slot_rows(b):
        b_copy(b).wait_recv()
        outs[b][1 - a] = backs[b][...]
        return jnp.concatenate([outs[b][0], outs[b][1]], axis=0)

    def chosen(pick, q, rows):
        mask = jnp.where(((lane >> 1) & 3) == q, pick[...], 0.0).astype(BF16)
        return jnp.dot(mask, rows, preferred_element_type=F32)

    def end_bwd():
        rows = slot_rows(0)
        tail = rows[:, quarter:]
        score_out[...] = chosen(pick_bwd, 0, tail) + chosen(pick_bwd, 2, tail)
        scale = scale_bwd[:, 0:1]
        factor = inverse[:, 0:1]
        products = jnp.zeros_like(scale)
        gain_own[...] = jnp.zeros_like(gain_own)
        for q in range(QUARTERS):
            grad = scale * chosen(pick_bwd, q, rows[:, :quarter])
            xhat = x_bwd[:, block(q)].astype(F32) * factor
            gain_own[q : q + 1, :] = jnp.sum(grad * xhat, axis=0, keepdims=True)
            products += jnp.sum(grad * gain[:, block(q)] * xhat, axis=1, keepdims=True)
        if pairs > 1:
            m_copy().start()
        average = products / (QUARTERS * quarter)
        for q in range(QUARTERS):
            grad = scale * chosen(pick_bwd, q, rows[:, :quarter])
            xhat = x_bwd[:, block(q)].astype(F32) * factor
            grad_x[:, block(q)] = (factor * (grad * gain[:, block(q)] - xhat * average)).astype(BF16)

    def end_fwd():
        rows = slot_rows(1)
        for q in range(QUARTERS):
            y_out[:, block(q)] = (scale_fwd[:, 0:1] * chosen(pick_fwd, q, rows)).astype(BF16)

    finish(0)
    finish(1)
    end_bwd()
    end_fwd()
    for b in range(2):
        b_copy(b).wait_send()
        x_copy(b).wait_send()
        own_sends(b, lambda c: c.wait_send())
    if pairs > 1:
        m_copy().wait()
        gain_out[...] = gain_own[...] + gain_came[...]
    else:
        gain_out[...] = gain_own[...] + gain_own[...]

    @pl.loop(1, half + 1)
    def _(t):
        for b in range(2):
            gather_step(b, t, False, lambda c: c.wait_send())
            reduce_drain(b, t)


def exchange(ring, *operands):
    packed_fwd, w_gate, x_bwd = operands[1], operands[3], operands[6]
    tokens = x_bwd.shape[0]
    quarter = packed_fwd.shape[2]
    hid = w_gate.shape[1]
    wide = quarter + EXTRA
    half = ring // 2
    slots = ring + half + 2
    rows_all = ring * 16
    vmem = pl.BlockSpec(memory_space=pltpu.VMEM)
    return pl.pallas_call(
        functools.partial(ring_kernel, ring),
        out_shape=(
            jax.ShapeDtypeStruct((tokens, QUARTERS * quarter), BF16),
            jax.ShapeDtypeStruct((tokens, QUARTERS * quarter), BF16),
            jax.ShapeDtypeStruct((tokens, EXTRA), F32),
            jax.ShapeDtypeStruct((8, quarter), F32),
        ),
        in_specs=[vmem] * 12,
        out_specs=(vmem,) * 4,
        scratch_shapes=[
            pltpu.VMEM((2, 16, wide), BF16),
            pltpu.VMEM((2, 16, quarter), BF16),
            pltpu.VMEM((8, quarter), F32),
            pltpu.VMEM((8, quarter), F32),
            pltpu.VMEM((tokens, EXTRA), F32),
            pltpu.VMEM((2, ring + half, 16, quarter), BF16),
            pltpu.VMEM((2, 16, quarter), BF16),
            pltpu.VMEM((rows_all, 2 * hid), F32),
            pltpu.VMEM((rows_all, 2 * hid * QUARTERS), BF16),
            pltpu.VMEM((ring, 16, wide), F32),
            pltpu.VMEM((ring, 16, quarter), F32),
            pltpu.VMEM((slots, 16, wide), BF16),
            pltpu.VMEM((slots, 16, quarter), BF16),
            pltpu.VMEM((16, wide), BF16),
            pltpu.VMEM((16, quarter), BF16),
            pltpu.VMEM((16, wide), BF16),
            pltpu.VMEM((16, quarter), BF16),
            pltpu.SemaphoreType.DMA((5,)),
            pltpu.SemaphoreType.DMA((5,)),
            pltpu.SemaphoreType.DMA((2, slots)),
            pltpu.SemaphoreType.DMA((2, slots)),
            pltpu.SemaphoreType.DMA((2, slots)),
            pltpu.SemaphoreType.DMA((2, slots)),
        ],
        compiler_params=pltpu.CompilerParams(
            collective_id=0, has_side_effects=True, vmem_limit_bytes=52 * 1024 * 1024
        ),
        cost_estimate=pl.CostEstimate(
            flops=24 * ring * 4 * quarter * 4 * hid, bytes_accessed=24 * quarter * hid, transcendentals=0
        ),
    )(*operands)


def per_device(
    forward_input_rows,
    ids_fwd,
    gate_fwd,
    backward_input_rows,
    dy_bwd,
    ids_bwd,
    gate_bwd,
    saved_z,
    norm_gain,
    w_gate,
    w_up,
    w_down,
):
    experts = 4
    ring = lax.axis_size("ep") // 2
    gain_vector_row = norm_gain[0]
    width = forward_input_rows.shape[2]
    hid = w_gate.shape[1]
    select_b, pick_gate_b, window = route_tables(ids_bwd[0], gate_bwd[0], experts)
    packed_bwd = pack_rows(select_b, dy_bwd[0])
    select_f, pick_gate_f, _ = route_tables(ids_fwd[0], gate_fwd[0], experts)
    xhat, _ = row_norm_values(forward_input_rows[0])
    packed_fwd = pack_rows(select_f, (xhat * gain_vector_row).astype(BF16))
    saved = saved_z[0].reshape(2, 2, ring, CAP, hid).transpose(0, 2, 1, 3, 4)
    saved = jnp.broadcast_to(saved.reshape(2, ring, 1, 2 * CAP, hid), (2, ring, 2, 2 * CAP, hid))
    saved = saved.reshape(2, ring * 8, hid).astype(F32)
    y_rows, grad_rows, score, gain_sum = exchange(
        ring,
        packed_bwd,
        packed_fwd,
        saved,
        w_gate,
        w_up,
        w_down,
        backward_input_rows[0],
        norm_gain,
        slot_picks(select_b),
        slot_picks(select_f),
        jnp.broadcast_to(pick_gate_b[:, None], (pick_gate_b.shape[0], EXTRA)),
        jnp.broadcast_to(pick_gate_f[:, None], (pick_gate_f.shape[0], EXTRA)),
    )
    grad_picks = jnp.where(window, score[:, 0:1], 0.0)[None]
    gain_sum = gain_sum[:QUARTERS].reshape(1, 1, width)
    return (y_rows[None], grad_rows[None], grad_picks, gain_sum)


def solution(mesh):
    rows = P("pp", "ep", None)
    return jax.shard_map(
        per_device,
        mesh=mesh,
        in_specs=(
            rows,
            rows,
            rows,
            rows,
            rows,
            rows,
            rows,
            P("pp", None, "ep", None),
            P("pp", None),
            P(None, "ep"),
            P(None, "ep"),
            P("ep", None),
        ),
        out_specs=(rows, rows, rows, rows),
        check_vma=False,
    )
```

```python
import functools

import jax
import jax.numpy as jnp
from jax import lax
from jax.experimental import pallas as pl
from jax.experimental.pallas import tpu as pltpu
from jax.sharding import PartitionSpec as P

EPSILON = 1e-06
QUARTERS = 4
EXTRA = 128
MESH = pl.DeviceIdType.MESH
F32 = jnp.float32
BF16 = jnp.bfloat16


def exact_pick(chooser, rows):
    return jnp.dot(chooser, rows, preferred_element_type=F32).astype(BF16)


def ring_kernel(
    ring,
    x_fwd,
    dy,
    ids_bwd,
    ids_fwd,
    gates_bwd,
    gates_fwd,
    gain,
    x_bwd_hbm,
    saved_hbm,
    w_gate_hbm,
    w_up_hbm,
    w_down_hbm,
    y_out,
    grad_x,
    score_out,
    gain_out,
    packed_bwd,
    packed_fwd,
    x_bwd,
    saved,
    w_gate,
    w_up,
    w_down,
    pick_bwd,
    pick_fwd,
    scale_bwd,
    scale_fwd,
    out_bwd,
    out_fwd,
    gain_own,
    gain_came,
    inverse,
    gathered,
    came_x,
    acc,
    lhs,
    part_bwd,
    part_fwd,
    sums_bwd,
    sums_fwd,
    back_bwd,
    back_fwd,
    fin_bwd,
    fin_fwd,
    x_send,
    x_recv,
    g_send,
    g_recv,
    r_send,
    r_recv,
    load,
):
    half = ring // 2
    pp = lax.axis_index("pp")
    ep = lax.axis_index("ep")
    a = ep // ring
    z = lax.rem(ep, ring)
    h = z // half
    i = lax.rem(z, half)
    quarter = packed_fwd.shape[2]
    hid = w_gate.shape[1]
    packed = (packed_bwd, packed_fwd)
    sums = (sums_bwd, sums_fwd)
    parts = (part_bwd, part_fwd)
    own_left, out_left = ring + half, ring + half + 1

    def at(position, pair=a):
        return (pp, pair * ring + lax.rem(position + 2 * ring, ring))

    partner = at(z, 1 - a)
    ways = (
        ((1, i, half), (-1, half - 1 - i, half - 1)),
        ((1, i, half - 1), (-1, half - 1 - i, half)),
    )

    loads = [
        pltpu.make_async_copy(source, target, load.at[n])
        for n, (source, target) in enumerate(
            (
                (x_bwd_hbm, x_bwd),
                (saved_hbm, saved),
                (w_down_hbm, w_down),
                (w_gate_hbm, w_gate),
                (w_up_hbm, w_up),
            )
        )
    ]
    for copy in loads:
        copy.start()

    barrier = pltpu.get_barrier_semaphore()
    pairs = lax.axis_size("pp")
    mirror = (pairs - 1 - pp, ep)
    for device in (at(z + 1), at(z - 1), partner) + ((mirror,) if pairs > 1 else ()):
        pl.semaphore_signal(barrier, inc=1, device_id=device, device_id_type=MESH)
    tokens = dy.shape[0]
    nt = (((1,), (1,)), ((), ()))

    def block(q):
        return slice(q * quarter, (q + 1) * quarter)

    def tables(ids, gates, pick, scale):
        slot = lax.broadcasted_iota(jnp.int32, (32, tokens), 0)
        hits = jnp.zeros((32, tokens), F32)
        for k in range(ids.shape[0]):
            hits += jnp.where(ids[k : k + 1, :] == (slot >> 3), 1.0, 0.0)
        from_t = lax.broadcasted_iota(jnp.int32, (tokens, tokens), 0)
        to_t = lax.broadcasted_iota(jnp.int32, (tokens, tokens), 1)
        earlier = jnp.where(from_t < to_t, 1.0, 0.0).astype(BF16)
        rank = jnp.dot(hits.astype(BF16), earlier, preferred_element_type=F32)
        by_slot = jnp.where(rank == (slot & 1).astype(F32), hits, 0.0)
        same = jnp.where(from_t == to_t, 1.0, 0.0).astype(BF16)
        pick[...] = lax.dot_general(same, by_slot.astype(BF16), nt, preferred_element_type=F32)
        gate = jnp.sum(jnp.where(ids[...] < 4, gates[...], 0.0), axis=0, keepdims=True)
        rest = jnp.broadcast_to(gate, (EXTRA, tokens))
        total = jnp.zeros((tokens, EXTRA), F32)
        for _ in range(3):
            high = rest.astype(BF16)
            total += lax.dot_general(same, high, nt, preferred_element_type=F32)
            rest = rest - high.astype(F32)
        scale[...] = total
        return by_slot

    def pack(b, by_slot, values):
        slot = lax.broadcasted_iota(jnp.int32, (32, 1), 0)
        total = jnp.zeros((32, quarter), F32)
        for q in range(QUARTERS):
            mask = jnp.where(((slot >> 1) & 3) == q, by_slot, 0.0).astype(BF16)
            total += jnp.dot(mask, values(q), preferred_element_type=F32)
        packed[b][0] = total[0:16].astype(BF16)
        packed[b][1] = total[16:32].astype(BF16)

    def root_scale(rows):
        squares = jnp.zeros((tokens, 1), F32)
        for q in range(QUARTERS):
            piece = rows[:, block(q)].astype(F32)
            squares += jnp.sum(piece * piece, axis=1, keepdims=True)
        return lax.rsqrt(squares / (QUARTERS * quarter) + EPSILON)

    pack(0, tables(ids_bwd, gates_bwd, pick_bwd, scale_bwd), lambda q: dy[:, block(q)])

    pl.semaphore_wait(barrier, 4 if pairs > 1 else 3)

    def x_copy(b):
        return pltpu.make_async_remote_copy(
            src_ref=packed[b].at[1 - a],
            dst_ref=came_x.at[b],
            send_sem=x_send.at[b],
            recv_sem=x_recv.at[b],
            device_id=partner,
            device_id_type=MESH,
        )

    x_copy(0).start()
    root = root_scale(x_fwd)
    pack(
        1,
        tables(ids_fwd, gates_fwd, pick_fwd, scale_fwd),
        lambda q: (x_fwd[:, block(q)].astype(F32) * root * gain[:, block(q)]).astype(BF16),
    )
    x_copy(1).start()

    def g_copy(b, source, target, sem, way):
        return pltpu.make_async_remote_copy(
            src_ref=gathered.at[b, source],
            dst_ref=gathered.at[b, target],
            send_sem=g_send.at[b, sem],
            recv_sem=g_recv.at[b, target],
            device_id=at(z + way),
            device_id_type=MESH,
        )

    def g_arrived(b, slot):
        g_copy(b, slot, slot, slot, 1).wait_recv()

    row = lax.broadcasted_iota(jnp.int32, (16, 32), 0)
    col = lax.broadcasted_iota(jnp.int32, (16, 32), 1)

    def merge(portion):
        pair = (row >> 1) & 1
        place = portion * 8 + (row >> 2) * 2 + (row & 1)
        return (col == jnp.where(pair == a, place, place + 16)).astype(BF16)

    def own_sends(b, act):
        for way, depth, reach in ways[b]:
            sem_in = z if way == 1 else own_left
            sem_out = ring + i if way == 1 else out_left

            @pl.when(depth >= half - reach)
            def _():
                act(g_copy(b, ring + i, jnp.where(depth < half - 1, ring + i, z), sem_out, way))

            @pl.when(depth < half - 1)
            def _():
                act(g_copy(b, z, z, sem_in, way))

    def begin(b):
        x_copy(b).wait_recv()
        rows = jnp.concatenate([packed[b][a], came_x[b]], axis=0)
        gathered[b, z] = exact_pick(merge(h), rows)
        gathered[b, ring + i] = exact_pick(merge(1 - h), rows)
        own_sends(b, lambda c: c.start())

    def gather_step(b, t, arrived, act):
        for way, depth, reach in ways[b]:
            source = lax.rem(z - way * t + ring, ring)

            @pl.when(t <= depth - half + reach)
            def _():
                slot = ring + i - way * t
                if arrived:
                    g_arrived(b, slot)
                act(g_copy(b, slot, jnp.where(depth < half - 1, slot, source), slot, way))

            @pl.when((t < reach) & (depth < half - 1))
            def _():
                if arrived:
                    g_arrived(b, source)
                act(g_copy(b, source, source, source, way))

    def gather_rest(b):
        for way, depth, reach in ways[b]:

            @pl.when(depth < half - 1)
            def _():
                g_arrived(b, lax.rem(z - way * reach + ring, ring))

            @pl.when(depth == half - 1)
            def _():
                @pl.loop(1, reach + 1)
                def _(t):
                    g_arrived(b, lax.rem(z - way * t + ring, ring))

    def r_copy(b, source, target, way):
        return pltpu.make_async_remote_copy(
            src_ref=sums[b].at[source],
            dst_ref=sums[b].at[target],
            send_sem=r_send.at[b, source],
            recv_sem=r_recv.at[b, target],
            device_id=at(z - way),
            device_id_type=MESH,
        )

    def r_arrived(b, slot):
        r_copy(b, slot, slot, 1).wait_recv()

    def rounded(b, total):
        if b == 1:
            return total.astype(BF16)
        score = total[0:8, quarter:] + total[8:16, quarter:]
        high = score.astype(BF16).astype(F32)
        tail = jnp.concatenate([high, score - high], axis=0)
        return jnp.concatenate([total[:, :quarter], tail], axis=1).astype(BF16)

    def reduce_step(b, t):
        for way, depth, reach in ways[b]:
            dest = lax.rem(z - way * t + ring, ring)
            local, other = dest, ring + lax.rem(dest, half)
            if way == -1:
                local = jnp.where(t == 1, own_left, local)
                other = jnp.where(t == 1, out_left, other)

            @pl.when(t <= reach)
            def _():
                chained = (t < reach) & (depth < half - 1)

                @pl.when(chained)
                def _():
                    r_arrived(b, dest)
                    sums[b][dest] = rounded(b, sums[b][dest].astype(F32) + parts[b][dest])

                @pl.when(jnp.logical_not(chained))
                def _():
                    sums[b][dest] = rounded(b, parts[b][dest])

                r_copy(b, dest, jnp.where(depth > 0, local, other), way).start()

            @pl.when(t <= depth - half + reach)
            def _():
                slot = ring + i - way * t
                r_arrived(b, slot)
                r_copy(b, slot, other, way).start()

    def reduce_drain(b, t):
        for way, depth, reach in ways[b]:
            dest = lax.rem(z - way * t + ring, ring)

            @pl.when(t <= reach)
            def _():
                r_copy(b, dest, dest, way).wait_send()

            @pl.when(t <= depth - half + reach)
            def _():
                slot = ring + i - way * t
                r_copy(b, slot, slot, way).wait_send()

    rows_all = ring * 16
    row_quarter = (lax.broadcasted_iota(jnp.int32, (rows_all, 1), 0) >> 2) & 3

    def folded(value):
        width = value.shape[1]
        pairs = value.reshape(ring, 2, 8, width)
        total = pairs[:, 0] + pairs[:, 1]
        total = total + pltpu.roll(total, 4, 1)
        return total.reshape(ring * 8, width)

    def spread(value):
        width = value.shape[1]
        tiles = value.reshape(ring, 1, 8, width)
        return jnp.concatenate([tiles, tiles], axis=1).reshape(rows_all, width)

    def saved_rows(n):
        place = lax.broadcasted_iota(jnp.int32, (ring * 8, ring * 4), 0)
        origin = lax.broadcasted_iota(jnp.int32, (ring * 8, ring * 4), 1)
        wanted = ((place >> 1) & 1) * (2 * ring) + (place >> 3) * 2 + (place & 1)
        mask = jnp.where(origin == wanted, 1.0, 0.0).astype(BF16)
        return jnp.dot(mask, saved[n], preferred_element_type=F32)

    def compute_bwd():
        rows = gathered[0, 0:ring].reshape(rows_all, quarter)
        for q in range(QUARTERS):
            piece = lax.dot_general(rows, w_down[:, block(q)], nt, preferred_element_type=F32)
            acc[:, :hid] = piece if q == 0 else jnp.where(row_quarter == q, piece, acc[:, :hid])
        grad_act = folded(acc[:, :hid])
        pre_gate = saved_rows(0)
        pre_up = saved_rows(1)
        sig = jax.nn.sigmoid(pre_gate)
        silu = pre_gate * sig
        active = (silu * pre_up).astype(BF16).astype(F32)
        grad_gate = grad_act * pre_up * sig * (1.0 + pre_gate * (1.0 - sig))
        grad_up = grad_act * silu
        score = jnp.sum(grad_act * active, axis=1, keepdims=True)
        score = jnp.broadcast_to(score, (ring * 8, EXTRA)).reshape(ring, 8, EXTRA)
        both = spread(jnp.concatenate([grad_gate, grad_up], axis=1))
        for q in range(QUARTERS):
            lhs[:, 2 * hid * q : 2 * hid * (q + 1)] = jnp.where(row_quarter == q, both, 0.0).astype(BF16)
        part_bwd[:, 0:8, quarter:] = score
        part_bwd[:, 8:16, quarter:] = jnp.zeros_like(score)
        for q in range(QUARTERS):
            weights = jnp.concatenate([w_gate[block(q), :], w_up[block(q), :]], axis=1)
            piece = lax.dot_general(
                lhs[:, 2 * hid * q : 2 * hid * (q + 1)], weights, nt, preferred_element_type=F32
            ).reshape(ring, 16, quarter)
            if q == 0:
                part_bwd[:, :, :quarter] = piece
            else:
                part_bwd[:, :, :quarter] += piece

    def compute_fwd():
        rows = gathered[1, 0:ring].reshape(rows_all, quarter)
        for q in range(QUARTERS):
            weights = jnp.concatenate([w_gate[block(q), :], w_up[block(q), :]], axis=1)
            piece = jnp.dot(rows, weights, preferred_element_type=F32)
            acc[...] = piece if q == 0 else jnp.where(row_quarter == q, piece, acc[...])
        z_both = folded(acc[...])
        z_gate = z_both[:, :hid]
        active = spread(z_gate * jax.nn.sigmoid(z_gate) * z_both[:, hid:])
        for q in range(QUARTERS):
            lhs[:, hid * q : hid * (q + 1)] = jnp.where(row_quarter == q, active, 0.0).astype(BF16)
        weights = jnp.concatenate([w_down[:, block(q)] for q in range(QUARTERS)], axis=0)
        part_fwd[...] = jnp.dot(
            lhs[:, : hid * QUARTERS], weights, preferred_element_type=F32
        ).reshape(ring, 16, quarter)

    begin(0)
    begin(1)
    for copy in loads:
        copy.wait()
    inverse[...] = jnp.broadcast_to(root_scale(x_bwd), inverse.shape)

    def send(copy):
        copy.start()

    gather_step(0, 1, True, send)

    @pl.loop(1, half)
    def _(t):
        gather_step(1, t, True, send)
        gather_step(0, t + 1, True, send)

    gather_rest(0)
    compute_bwd()
    gather_step(1, half, True, send)
    reduce_step(0, half)
    gather_rest(1)
    compute_fwd()

    @pl.loop(0, half - 1)
    def _(k):
        reduce_step(1, half - k)
        reduce_step(0, half - 1 - k)

    reduce_step(1, 1)

    backs = (back_bwd, back_fwd)
    fins = (fin_bwd, fin_fwd)
    outs = (out_bwd, out_fwd)

    def b_copy(b):
        return pltpu.make_async_remote_copy(
            src_ref=fins[b],
            dst_ref=backs[b],
            send_sem=x_send.at[2 + b],
            recv_sem=x_recv.at[2 + b],
            device_id=partner,
            device_id_type=MESH,
        )

    def compact(pair):
        place = (row & 1) + ((row >> 1) & 3) * 4 + pair * 2
        return (col == jnp.where((row >> 3) == h, place, place + 16)).astype(BF16)

    def finish(b):
        @pl.when(i < half - 1)
        def _():
            r_arrived(b, z)
            parts[b][z] += sums[b][z].astype(F32)

        @pl.when(i > 0)
        def _():
            r_arrived(b, own_left)
            parts[b][z] += sums[b][own_left].astype(F32)

        if b == 0:
            first, second, both = ring + i, out_left, i < half - 1
        else:
            first, second, both = out_left, ring + i, i > 0
        r_arrived(b, first)

        @pl.when(both)
        def _():
            r_arrived(b, second)
            added = sums[b][first].astype(F32) + sums[b][second].astype(F32)
            sums[b][first] = rounded(b, added)

        rows = jnp.concatenate([rounded(b, parts[b][z]), sums[b][first]], axis=0)
        fins[b][...] = exact_pick(compact(1 - a), rows)
        b_copy(b).start()
        outs[b][a] = exact_pick(compact(a), rows)

    def m_copy():
        return pltpu.make_async_remote_copy(
            src_ref=gain_own,
            dst_ref=gain_came,
            send_sem=x_send.at[4],
            recv_sem=x_recv.at[4],
            device_id=mirror,
            device_id_type=MESH,
        )

    lane = lax.broadcasted_iota(jnp.int32, (1, 32), 1)

    def slot_rows(b):
        b_copy(b).wait_recv()
        outs[b][1 - a] = backs[b][...]
        return jnp.concatenate([outs[b][0], outs[b][1]], axis=0)

    def chosen(pick, q, rows):
        mask = jnp.where(((lane >> 1) & 3) == q, pick[...], 0.0).astype(BF16)
        return jnp.dot(mask, rows, preferred_element_type=F32)

    def end_bwd():
        rows = slot_rows(0)
        tail = rows[:, quarter:]
        score_out[...] = chosen(pick_bwd, 0, tail) + chosen(pick_bwd, 2, tail)
        scale = scale_bwd[:, 0:1]
        factor = inverse[:, 0:1]
        products = jnp.zeros_like(scale)
        gain_own[...] = jnp.zeros_like(gain_own)
        for q in range(QUARTERS):
            grad = scale * chosen(pick_bwd, q, rows[:, :quarter])
            xhat = x_bwd[:, block(q)].astype(F32) * factor
            gain_own[q : q + 1, :] = jnp.sum(grad * xhat, axis=0, keepdims=True)
            products += jnp.sum(grad * gain[:, block(q)] * xhat, axis=1, keepdims=True)
        if pairs > 1:
            m_copy().start()
        average = products / (QUARTERS * quarter)
        for q in range(QUARTERS):
            grad = scale * chosen(pick_bwd, q, rows[:, :quarter])
            xhat = x_bwd[:, block(q)].astype(F32) * factor
            grad_x[:, block(q)] = (factor * (grad * gain[:, block(q)] - xhat * average)).astype(BF16)

    def end_fwd():
        rows = slot_rows(1)
        for q in range(QUARTERS):
            y_out[:, block(q)] = (scale_fwd[:, 0:1] * chosen(pick_fwd, q, rows)).astype(BF16)

    finish(0)
    finish(1)
    end_bwd()
    end_fwd()
    for b in range(2):
        b_copy(b).wait_send()
        x_copy(b).wait_send()
        own_sends(b, lambda c: c.wait_send())
    if pairs > 1:
        m_copy().wait()
        gain_out[...] = gain_own[...] + gain_came[...]
    else:
        gain_out[...] = gain_own[...] + gain_own[...]

    @pl.loop(1, half + 1)
    def _(t):
        for b in range(2):
            gather_step(b, t, False, lambda c: c.wait_send())
            reduce_drain(b, t)


def exchange(ring, *operands):
    x_fwd, saved, w_gate, w_down = operands[0], operands[8], operands[9], operands[11]
    tokens, width = x_fwd.shape
    quarter = width // QUARTERS
    hid = w_gate.shape[1]
    wide = quarter + EXTRA
    half = ring // 2
    slots = ring + half + 2
    rows_all = ring * 16
    vmem = pl.BlockSpec(memory_space=pltpu.VMEM)
    return pl.pallas_call(
        functools.partial(ring_kernel, ring),
        out_shape=(
            jax.ShapeDtypeStruct((tokens, QUARTERS * quarter), BF16),
            jax.ShapeDtypeStruct((tokens, QUARTERS * quarter), BF16),
            jax.ShapeDtypeStruct((tokens, EXTRA), F32),
            jax.ShapeDtypeStruct((8, quarter), F32),
        ),
        in_specs=[vmem] * 7 + [pl.BlockSpec(memory_space=pl.ANY)] * 5,
        out_specs=(vmem,) * 4,
        scratch_shapes=[
            pltpu.VMEM((2, 16, quarter), BF16),
            pltpu.VMEM((2, 16, quarter), BF16),
            pltpu.VMEM((tokens, width), BF16),
            pltpu.VMEM(saved.shape, BF16),
            pltpu.VMEM(w_gate.shape, BF16),
            pltpu.VMEM(w_gate.shape, BF16),
            pltpu.VMEM(w_down.shape, BF16),
            pltpu.VMEM((tokens, 32), F32),
            pltpu.VMEM((tokens, 32), F32),
            pltpu.VMEM((tokens, EXTRA), F32),
            pltpu.VMEM((tokens, EXTRA), F32),
            pltpu.VMEM((2, 16, wide), BF16),
            pltpu.VMEM((2, 16, quarter), BF16),
            pltpu.VMEM((8, quarter), F32),
            pltpu.VMEM((8, quarter), F32),
            pltpu.VMEM((tokens, EXTRA), F32),
            pltpu.VMEM((2, ring + half, 16, quarter), BF16),
            pltpu.VMEM((2, 16, quarter), BF16),
            pltpu.VMEM((rows_all, 2 * hid), F32),
            pltpu.VMEM((rows_all, 2 * hid * QUARTERS), BF16),
            pltpu.VMEM((ring, 16, wide), F32),
            pltpu.VMEM((ring, 16, quarter), F32),
            pltpu.VMEM((slots, 16, wide), BF16),
            pltpu.VMEM((slots, 16, quarter), BF16),
            pltpu.VMEM((16, wide), BF16),
            pltpu.VMEM((16, quarter), BF16),
            pltpu.VMEM((16, wide), BF16),
            pltpu.VMEM((16, quarter), BF16),
            pltpu.SemaphoreType.DMA((5,)),
            pltpu.SemaphoreType.DMA((5,)),
            pltpu.SemaphoreType.DMA((2, slots)),
            pltpu.SemaphoreType.DMA((2, slots)),
            pltpu.SemaphoreType.DMA((2, slots)),
            pltpu.SemaphoreType.DMA((2, slots)),
            pltpu.SemaphoreType.DMA((5,)),
        ],
        compiler_params=pltpu.CompilerParams(
            collective_id=0, has_side_effects=True, vmem_limit_bytes=52 * 1024 * 1024
        ),
        cost_estimate=pl.CostEstimate(
            flops=24 * ring * 4 * quarter * 4 * hid, bytes_accessed=24 * quarter * hid, transcendentals=0
        ),
    )(*operands)


def per_device(
    forward_input_rows,
    ids_fwd,
    gate_fwd,
    backward_input_rows,
    dy_bwd,
    ids_bwd,
    gate_bwd,
    saved_z,
    norm_gain,
    w_gate,
    w_up,
    w_down,
):
    ring = lax.axis_size("ep") // 2
    width = forward_input_rows.shape[2]
    window = ids_bwd[0] < 4
    y_rows, grad_rows, score, gain_sum = exchange(
        ring,
        forward_input_rows[0],
        dy_bwd[0],
        ids_bwd[0].T,
        ids_fwd[0].T,
        gate_bwd[0].T,
        gate_fwd[0].T,
        norm_gain,
        backward_input_rows[0],
        saved_z[0],
        w_gate,
        w_up,
        w_down,
    )
    grad_picks = jnp.where(window, score[:, 0:1], 0.0)[None]
    gain_sum = gain_sum[:QUARTERS].reshape(1, 1, width)
    return (y_rows[None], grad_rows[None], grad_picks, gain_sum)


def solution(mesh):
    rows = P("pp", "ep", None)
    return jax.shard_map(
        per_device,
        mesh=mesh,
        in_specs=(
            rows,
            rows,
            rows,
            rows,
            rows,
            rows,
            rows,
            P("pp", None, "ep", None),
            P("pp", None),
            P(None, "ep"),
            P(None, "ep"),
            P("ep", None),
        ),
        out_specs=(rows, rows, rows, rows),
        check_vma=False,
    )
```
